512 devices in a mesh: row: 16 (over z, core), col: 32 (over x, y).
Axes of the slice: x: 4, y: 8, z: 8, core: 2. Of those that a mesh axis runs over, the one named last changes fastest.
Arguments:
- front: float32 [12288, 12288], P('row', 'col'), as said below
- structure: int32 [3, 96], replicated, may hold values from 0 to 1, as said below
- factor_front: float32 [3, 12288, 512], P(None, 'row', 'col'), may hold values from -0.0546875 to 0.0546875
- factor_border: float32 [2, 512, 512], replicated, may hold values from -0.6 to 0.6
- pivot_inverse: float32 [3, 512, 512], P(None, 'row')
Outputs:
- inverse_front: float32 [3, 512, 12288], P(None, 'row', 'col')
- inverse_parent: float32 [2, 512, 512], P(None, 'row')
- inverse_diagonal: float32 [3, 512, 512], P(None, 'row')
The draws below stay inside these ranges and needn't reach their ends.
Inputs may be any that keep to these rules, and one draw needn't show every extreme that they name: front is exactly symmetric. structure[k, b] = 1 where front block b (rows b * 128 to (b + 1) * 128 - 1) lies in supernode k's structure; every 1 in row k is also a 1 in row k - 1; blocks b < 24 are 1 in every row.
All inputs are finite; a program needn't handle non-finite values.
Results may differ from the reference program's by a relative error of at most 0.0001.
Values sent between devices are 32-bit elements; how exact they have to be, the bound alone decides.
A program may use at most 64 MiB of HBM per device.

```python
import jax
import jax.numpy as jnp
from jax import lax

F = 12288
W = 512
BLK = 128
SUPER = 3
NBLK = 96


def draw_front(key, part):
    noise_part = jax.random.normal(jax.random.fold_in(key, 11), (F, F), jnp.float32) * 0.02
    symmetric = (noise_part + noise_part.T) * 0.5
    diagonal = jnp.exp(jax.random.uniform(jax.random.fold_in(key, 12), (F,), jnp.float32, jnp.log(4.0), jnp.log(16.0)))
    return symmetric + jnp.diag(diagonal)


def draw_pivot_inverse(key, part):
    noise_part = jax.random.normal(jax.random.fold_in(key, 31), (SUPER, W, W), jnp.float32) * (0.5 / W ** 0.5)
    symmetric = (noise_part + jnp.swapaxes(noise_part, 1, 2)) * 0.5
    diagonal = jnp.exp(jax.random.uniform(jax.random.fold_in(key, 32), (SUPER, W), jnp.float32, jnp.log(1.0), jnp.log(4.0)))
    return symmetric + diagonal[:, :, None] * jnp.eye(W, dtype=jnp.float32)[None, :, :]


def draw_structure(key, part):
    draws = jax.random.randint(jax.random.fold_in(key, 21), (NBLK,), 0, 1000)
    numbers = jnp.arange(NBLK, dtype=jnp.int32)
    levels = 200 + 700 * numbers // NBLK
    sections = jnp.arange(SUPER, dtype=jnp.int32)
    listed = draws[None, :] * (SUPER + 1) < levels[None, :] * (SUPER + 1 - sections[:, None])
    forced = (numbers < NBLK // 4)[None, :]
    return jnp.logical_or(listed, forced).astype(jnp.int32)


def block_scale(rng, shape, pieces, smallest, top_value):
    factor_of = 1.0
    for axis_at, shards_of in pieces:
        steps = jax.random.uniform(jax.random.fold_in(jax.random.fold_in(rng, 6), axis_at), (shards_of,), jnp.float32, smallest / len(pieces), top_value / len(pieces))
        factor_of = factor_of * jnp.repeat(jnp.exp(steps), shape[axis_at] // shards_of).reshape((-1,) + (1,) * (len(shape) - 1 - axis_at))
    return factor_of


def noise(own_key, extent, spread, limit, pieces=(), kind=jnp.bfloat16):
    loudness = block_scale(own_key, extent, pieces, -0.22, 0.18) if pieces else 1.0
    array = jax.random.normal(own_key, extent, jnp.float32) * spread * loudness
    return jnp.minimum(jnp.maximum(array, -limit), limit).astype(kind)


def setup_inputs(seed: int = 0) -> dict:
    streams_of = jax.random.split(jax.random.key(seed), 6)
    front = draw_front(jax.random.fold_in(streams_of[5], 71), 0)
    structure = draw_structure(jax.random.fold_in(streams_of[5], 71), 0)
    factor_front = noise(streams_of[2], (SUPER, F, W), F ** -0.5, 0.0546875, ((1, 16), (2, 32)), jnp.float32)
    factor_border = noise(streams_of[3], (SUPER - 1, W, W), 0.1, 0.6, (), jnp.float32)
    pivot_inverse = draw_pivot_inverse(jax.random.fold_in(streams_of[5], 71), 0)
    return dict(front=front, structure=structure, factor_front=factor_front, factor_border=factor_border, pivot_inverse=pivot_inverse)


HIGH = lax.Precision.HIGHEST


def matmul(former, latter):
    return jnp.dot(former, latter, precision=HIGH, preferred_element_type=jnp.float32)


def reference(front, structure, factor_front, factor_border, pivot_inverse):
    supers = structure.shape[0]
    order = front.shape[0]
    owners = (jnp.arange(order, dtype=jnp.int32) // BLK).astype(jnp.int32)
    fronts = []
    parents = []
    diagonals = []
    previous = None
    diag_prev = None
    for section in range(supers):
        flags = structure[section][owners].astype(jnp.float32)
        factor_rows = factor_front[section] * flags[:, None]
        image = matmul(front, factor_rows)
        if section > 0:
            border = factor_border[section - 1]
            image = image + matmul(previous, border)
            parent = matmul(previous.T, factor_rows) + matmul(diag_prev, border)
            parents.append(-parent)
        current = -(image * flags[:, None])
        diag_now = pivot_inverse[section] + matmul(image.T, factor_rows)
        if section > 0:
            diag_now = diag_now + matmul(parent.T, border)
        fronts.append(current.T)
        diagonals.append(diag_now)
        previous = current
        diag_prev = diag_now
    return jnp.stack(fronts), jnp.stack(parents), jnp.stack(diagonals)
```

```python
import functools

import jax
import jax.numpy as jnp
from jax import lax
from jax.experimental import pallas as pl
from jax.experimental.pallas import tpu as pltpu
from jax.sharding import PartitionSpec as P

NX, NY, NZ = 4, 8, 8
SIZES = (NX, NY)
SUPER = 3
BLK = 128
PIECES = 4
AG_DELAY = (0, 3, 6)
BC_START = (0, 6, 12)
MESH = pl.DeviceIdType.MESH
F32 = jnp.float32


def gather_plan():
    msgs = []
    for first in range(2):
        n1, n2 = SIZES[first], SIZES[1 - first]
        for j in range(1, n1 // 2 + 1):
            for s in (1, -1):
                msgs.append((j, first, s, j, None, 0))
        for o in range(-(n1 // 2) + 1, n1 // 2 + 1):
            for i in range(1, n2 // 2 + 1):
                for s in (1, -1):
                    msgs.append((abs(o) + i, first, 0, o, s, i))
    return msgs


MSGS = gather_plan()
INDEX = {m[1:]: i for i, m in enumerate(MSGS)}
BY_KEY = {m[1:]: m for m in MSGS}


def wrap(v, n):
    return lax.rem(v + n, n)


def split(v):
    high = v.astype(jnp.bfloat16)
    low = (v - high.astype(F32)).astype(jnp.bfloat16)
    return high, low


NN = (((1,), (0,)), ((), ()))
NT = (((1,), (1,)), ((), ()))


def dot3(a, b, dims=NN):
    def one(p, q):
        return lax.dot_general(p, q, dims, preferred_element_type=F32)
    return one(a[0], b[0]) + (one(a[0], b[1]) + one(a[1], b[0]))


def kernel(flag_ref, a_ref, f_ref, b_ref, p_ref, x_out, par_out, d_out,
           FA, FB, PF, Yp, E, RB, Hc, Ah, Al, Bh, Bl, BTh, BTl, Hh, Hl, Yr, TP, R1, R2, R3, TF, U, Q,
           ag_s, ag_r, pz_s, pz_r, ex_s, ex_r, rs_s, rs_r, bc_s, bc_r, rt_s, rt_r, sx_s, sx_r, cp_s,
           t1_s, t1_r, t2_s, t2_r, t3_s, t3_r):
    row = lax.axis_index("row")
    col = lax.axis_index("col")
    z, core = lax.div(row, 2), lax.rem(row, 2)
    x, y = lax.div(col, NY), lax.rem(col, NY)
    other = 1 - core

    def at(dx=0, dy=0, dz=0):
        return (wrap(z + dz, NZ) * 2 + core, wrap(x + dx, NX) * NY + wrap(y + dy, NY))

    sibling = (z * 2 + other, col)

    def remote(src, dst, s_sem, r_sem, dev):
        return pltpu.make_async_remote_copy(
            src_ref=src, dst_ref=dst, send_sem=s_sem, recv_sem=r_sem, device_id=dev, device_id_type=MESH)

    sends = []

    def start(c):
        c.start()
        sends.append(c)

    barrier = pltpu.get_barrier_semaphore()
    peers = [at(dx=o) for o in range(1, NX)] + [at(dy=o) for o in range(1, NY)]
    peers += [at(dz=1), at(dz=-1), sibling]
    for dev in peers:
        pl.semaphore_signal(barrier, inc=1, device_id=dev, device_id_type=MESH)

    for k in range(SUPER):
        for j in range(6):
            flag = flag_ref[k, row * 6 + j].astype(F32)
            dst = (FA, FB)[j // 3]
            dst[k, x, y, :, (j % 3) * BLK:(j % 3 + 1) * BLK] = f_ref[k, :, j * BLK:(j + 1) * BLK] * flag
    PF[:, z, core] = p_ref[0:2]
    pl.semaphore_wait(barrier, len(peers))

    def ag_copy(k, key, back):
        first, s1, o, s2, i = key
        n1, n2 = SIZES[first], SIZES[1 - first]
        F = (FA, FB)[first]
        if s2 is None:
            half, s = o == n1 // 2, s1
            off1, off2 = -s1 * (o - 1 + back), 0
            step = (s, 0)
        else:
            half, s = i == n2 // 2, s2
            off1, off2 = o, -s2 * (i - 1 + back)
            step = (0, s)
        rows = pl.ds(0 if s > 0 else 8, 8) if half else pl.ds(0, 16)
        if first == 1:
            off1, off2 = off2, off1
            step = step[::-1]
        ref = F.at[k, wrap(x + off1, NX), wrap(y + off2, NY), rows]
        n = k * len(MSGS) + INDEX[key]
        return remote(ref, ref, ag_s.at[n], ag_r.at[n], at(*step))

    def ag_second(k, first, o):
        o = o if o > -(SIZES[first] // 2) else -o
        for s in (1, -1):
            start(ag_copy(k, (first, 0, o, s, 1), 0))

    def ag_begin(k):
        for first in range(2):
            for s in (1, -1):
                start(ag_copy(k, (first, s, 1, None, 0), 0))
        for first in range(2):
            ag_second(k, first, 0)

    def ag_arrive(k, m):
        key = m[1:]
        ag_copy(k, key, 1).wait_recv()
        first, s1, o, s2, i = key
        n1, n2 = SIZES[first], SIZES[1 - first]
        if s2 is None:
            if o < n1 // 2:
                start(ag_copy(k, (first, s1, o + 1, None, 0), 0))
                ag_second(k, first, -s1 * o)
            elif s1 < 0:
                ag_second(k, first, o)
        elif i < n2 // 2:
            start(ag_copy(k, (first, 0, o, s2, i + 1), 0))

    def ag_tick(k, t):
        for m in sorted((m for m in MSGS if m[0] == t), key=lambda m: (m[4] is not None, m[5])):
            ag_arrive(k, m)

    def pz_copy(s, t, back):
        half = t == NZ // 2
        rows = pl.ds(0 if s > 0 else 16, 16) if half else pl.ds(0, 32)
        ref = PF.at[:, wrap(z - s * (t - 1 + back), NZ), core, rows]
        n = (t - 1) * 2 + (s > 0)
        return remote(ref, ref, pz_s.at[n], pz_r.at[n], at(dz=s))

    def pz_tick(t):
        for s in (1, -1):
            if t > 0:
                pz_copy(s, t, 1).wait_recv()
            if t < NZ // 2:
                start(pz_copy(s, t + 1, 0))

    def pz_pair(side):
        ref = PF.at[:, :, side]
        return remote(ref, ref, pz_s.at[8], pz_r.at[8], sibling)

    def prepare():
        Ah[...], Al[...] = split(a_ref[...])
        for i in range(2):
            b = b_ref[i]
            Bh[i], Bl[i] = split(b)
            BTh[i], BTl[i] = split(b.T)

    def product(k):
        for h in range(2):
            out = None
            for F, base in ((FA, 0), (FB, 384)):
                left = split(F[k, 2 * h:2 * h + 2].reshape(256, 384))
                term = dot3(left, (Ah[base:base + 384], Al[base:base + 384]))
                out = term if out is None else out + term
            if k > 0:
                rows = slice(h * 256, h * 256 + 256)
                before = split(Yp[k - 1].reshape(512, 384))
                out = out - dot3((BTh[k - 1, rows], BTl[k - 1, rows]), before)
            Yp[k, 4 * h:4 * h + 4] = out.reshape(4, 2, 32, 384)

    def ex_copy(k):
        return remote(Yp.at[k, :, other], E.at[k], ex_s.at[k], ex_r.at[k], sibling)

    def ex_finish(k):
        ex_copy(k).wait_recv()
        E[k] = E[k] + Yp[k, :, core]

    def rs_rows(s, t):
        return (pl.ds(0, 16) if s > 0 else pl.ds(16, 16)) if t == 1 else pl.ds(0, 32)

    def rs_copy(k, s, t):
        n = (k * 4 + t - 1) * 2 + (s > 0)
        rows = rs_rows(s, t)
        return remote(E.at[k, wrap(z + s * (5 - t), NZ), rows], RB.at[k, int(s > 0), t - 1, rows],
                      rs_s.at[n], rs_r.at[n], at(dz=s))

    def rs_tick(k, t):
        for s in (1, -1):
            if t > 0:
                rs_copy(k, s, t).wait_recv()
                rows = rs_rows(s, t)
                block = wrap(z + s * (4 - t), NZ)
                E[k, block, rows] = E[k, block, rows] + RB[k, int(s > 0), t - 1, rows]
            if t < 4:
                start(rs_copy(k, s, t + 1))

    def columns_out(k):
        image = E[k, z]
        Yr[k] = image
        for j in range(3):
            flag = flag_ref[k, col * 3 + j].astype(F32)
            lanes = slice(j * BLK, (j + 1) * BLK)
            x_out[k, :, lanes] = -(image[:, lanes] * flag)

    root_z = lax.div(col, 4)
    root_core = lax.rem(lax.div(col, 2), 2)
    in_root_plane = z == root_z
    is_root = jnp.logical_and(in_root_plane, core == root_core)
    even = lax.rem(col, 2) == 0

    def root_copies(k):
        for F, mine in ((FA, even), (FB, jnp.logical_not(even))):
            yield (pltpu.make_async_copy(F.at[k], Hc.at[k], cp_s.at[k]),
                   remote(F.at[k], Hc.at[k], rt_s.at[k], rt_r.at[k], sibling),
                   jnp.logical_and(is_root, mine))

    def bc_root(k):
        for local, away, here in root_copies(k):
            @pl.when(here)
            def _():
                away.start()
                local.start()
                local.wait()

        @pl.when(jnp.logical_and(in_root_plane, core != root_core))
        def _():
            remote(Hc.at[k], Hc.at[k], rt_s.at[k], rt_r.at[k], sibling).wait_recv()

    def bc_root_done(k):
        for local, away, here in root_copies(k):
            @pl.when(here)
            def _():
                away.wait_send()

    def bc_copy(k, s, p):
        n = (k * 2 + (s > 0)) * PIECES + p
        w = NY // PIECES
        ref = Hc.at[k, 2 * core + (s > 0), pl.ds(p * w, w)]
        return remote(ref, ref, bc_s.at[n], bc_r.at[n], at(dz=s))

    def bc_place(s):
        return wrap(s * (z - root_z) + NZ, NZ)

    def bc_slot(slot):
        for k in range(SUPER):
            if not 0 <= slot - BC_START[k] < NZ - 1 + PIECES:
                continue
            for s in (1, -1):
                place = bc_place(s)
                p = slot - BC_START[k] - place
                there = jnp.logical_and(p >= 0, p < PIECES)

                @pl.when(jnp.logical_and(there, place > 0))
                def _():
                    bc_copy(k, s, p).wait_recv()

                @pl.when(jnp.logical_and(there, place < NZ - 1))
                def _():
                    bc_copy(k, s, p).start()

    def bc_done(k):
        for p in range(PIECES):
            for s in (1, -1):
                @pl.when(bc_place(s) < NZ - 1)
                def _():
                    bc_copy(k, s, p).wait_send()

    def bc_pair(k, side):
        ref = Hc.at[k, pl.ds(2 * side, 2)]
        return remote(ref, ref, sx_s.at[k], sx_r.at[k], sibling)

    def bc_swap(k):
        @pl.when(jnp.logical_not(in_root_plane))
        def _():
            bc_pair(k, core).start()

    def bc_swapped(k):
        @pl.when(jnp.logical_not(in_root_plane))
        def _():
            bc_pair(k, other).wait_recv()
            bc_pair(k, core).wait_send()

    def reduced_factor(k):
        h = Hc[k].reshape(512, 384)
        if k > 0:
            h = h - dot3((BTh[k - 1], BTl[k - 1]), (Hh[k - 1], Hl[k - 1]))
        Hh[k], Hl[k] = split(h)

    def gram(k):
        if k == 0:
            TP[0:32] = dot3(split(Yr[0]), (Hh[0], Hl[0]), NT)
        else:
            left = Yr[k - 1:k + 1].reshape(64, 384)
            TP[64 * k - 32:64 * k + 32] = dot3(split(left), (Hh[k], Hl[k]), NT)

    def piece_of(ref, at_y):
        return ref.at[pl.ds(pl.multiple_of(lax.div(at_y, 2) * 40, 8), 40),
                      pl.ds(pl.multiple_of(lax.rem(at_y, 2) * 256, 256), 256)]

    def t_sum():
        c1 = [remote(piece_of(TP, wrap(y + o, NY)), R1.at[o], t1_s.at[o], t1_r.at[o], at(dy=o)) for o in range(1, NY)]
        for c in c1:
            start(c)
        own = piece_of(TP, y)[...]
        for o in range(1, NY):
            c1[o - 1].wait_recv()
            own = own + R1[o]
        R2[0] = own
        c2 = [remote(R2.at[0], R2.at[o], t2_s.at[o], t2_r.at[o], at(dx=o)) for o in range(1, NX)]
        for c in c2:
            start(c)
        for c in c2:
            c.wait_recv()
        total = R2[wrap(x, NX)]
        for i in range(1, NX):
            total = total + R2[wrap(x - i + NX, NX)]
        R3[...] = total
        c3 = [remote(R3, piece_of(TF, y), t3_s.at[o], t3_r.at[o], at(dy=o)) for o in range(1, NY)]
        for c in c3:
            start(c)
        piece_of(TF, y)[...] = total
        for o in range(1, NY):
            piece = piece_of(TF, wrap(y - o, NY))
            remote(piece, piece, t3_s.at[o], t3_r.at[o], at(dy=o)).wait_recv()

    def pivot_terms():
        b0, b1 = (Bh[0], Bl[0]), (Bh[1], Bl[1])
        mine = pl.ds(pl.multiple_of(row * 32, 32), 32)
        bt0, bt1 = (BTh[0, mine], BTl[0, mine]), (BTh[1, mine], BTl[1, mine])
        p0, p1 = split(PF[0].reshape(512, 512)), split(PF[1].reshape(512, 512))
        own0, own1, own2 = p_ref[0], p_ref[1], p_ref[2]
        q1 = own1 + dot3(split(dot3(bt0, p0, NT)), b0)
        U[0] = dot3(split(own0), b0)
        U[1] = dot3(split(q1), b1)
        inner = dot3(split(dot3(split(dot3(bt1, b0, NT)), p0)), b0) + dot3(bt1, p1, NT)
        Q[0] = q1
        Q[1] = own2 + dot3(split(inner), b1)

    def ag_step(g):
        for k in range(SUPER):
            if g == AG_DELAY[k]:
                ag_begin(k)
            elif 0 < g - AG_DELAY[k] <= 6:
                ag_tick(k, g - AG_DELAY[k])

    def slots(*numbers):
        for n in numbers:
            bc_slot(n)

    ag_step(0)
    pz_tick(0)
    prepare()
    for g in range(1, 6):
        ag_step(g)
        if g <= 4:
            pz_tick(g)
        if g == 4:
            start(pz_pair(core))
    ag_step(6)
    bc_root(0)
    slots(0)
    product(0)
    start(ex_copy(0))
    slots(1, 2)
    ag_step(7)
    slots(3, 4)
    ex_finish(0)
    rs_tick(0, 0)
    ag_step(8)
    slots(5)
    rs_tick(0, 1)
    ag_step(9)
    bc_root(1)
    slots(6)
    product(1)
    start(ex_copy(1))
    slots(7)
    rs_tick(0, 2)
    ag_step(10)
    slots(8, 9)
    rs_tick(0, 3)
    ex_finish(1)
    rs_tick(1, 0)
    ag_step(11)
    slots(10, 11)
    rs_tick(0, 4)
    bc_swap(0)
    rs_tick(1, 1)
    ag_step(12)
    bc_root(2)
    slots(12)
    product(2)
    start(ex_copy(2))
    slots(13)
    rs_tick(1, 2)
    slots(14)
    ex_finish(2)
    rs_tick(2, 0)
    rs_tick(1, 3)
    columns_out(0)
    bc_swapped(0)
    reduced_factor(0)
    slots(15)
    rs_tick(2, 1)
    rs_tick(1, 4)
    slots(16)
    bc_swap(1)
    columns_out(1)
    gram(0)
    slots(17)
    rs_tick(2, 2)
    slots(18)
    bc_swapped(1)
    reduced_factor(1)
    slots(19)
    rs_tick(2, 3)
    slots(20)
    gram(1)
    slots(21)
    rs_tick(2, 4)
    slots(22)
    bc_swap(2)
    columns_out(2)
    pz_pair(other).wait_recv()
    pivot_terms()
    bc_swapped(2)
    reduced_factor(2)
    gram(2)
    t_sum()
    d_out[0] = p_ref[0] + TF[0:32]
    d_out[1] = Q[0] + TF[64:96]
    d_out[2] = Q[1] + TF[128:160]
    par_out[0] = TF[32:64] - U[0]
    par_out[1] = TF[96:128] - U[1]
    for c in sends:
        c.wait_send()
    for k in range(SUPER):
        bc_root_done(k)
        bc_done(k)


def body(front, structure, factor_front, factor_border, pivot_inverse):
    vmem = pl.BlockSpec(memory_space=pltpu.VMEM)
    dma = lambda n: pltpu.SemaphoreType.DMA((n,))
    v = lambda *shape: pltpu.VMEM(shape, F32)
    h = lambda *shape: pltpu.VMEM(shape, jnp.bfloat16)
    n_ag = SUPER * len(MSGS)
    return pl.pallas_call(
        kernel,
        out_shape=(
            jax.ShapeDtypeStruct((3, 32, 384), F32),
            jax.ShapeDtypeStruct((2, 32, 512), F32),
            jax.ShapeDtypeStruct((3, 32, 512), F32),
        ),
        in_specs=[pl.BlockSpec(memory_space=pltpu.SMEM)] + [vmem] * 4,
        out_specs=(vmem,) * 3,
        scratch_shapes=[
            v(3, NX, NY, 16, 384), v(3, NX, NY, 16, 384),
            v(2, NZ, 2, 32, 512),
            v(3, NZ, 2, 32, 384),
            v(3, NZ, 32, 384),
            v(3, 2, 4, 32, 384),
            v(3, NX, NY, 16, 384),
            h(768, 384), h(768, 384),
            h(2, 512, 512), h(2, 512, 512), h(2, 512, 512), h(2, 512, 512),
            h(3, 512, 384), h(3, 512, 384),
            v(3, 32, 384),
            v(160, 512),
            v(NY, 40, 256), v(NX, 40, 256), v(40, 256),
            v(160, 512),
            v(2, 32, 512), v(2, 32, 512),
            dma(n_ag), dma(n_ag),
            dma(9), dma(9),
            dma(3), dma(3),
            dma(24), dma(24),
            dma(6 * PIECES), dma(6 * PIECES),
            dma(3), dma(3),
            dma(3), dma(3),
            dma(3),
            dma(NY), dma(NY), dma(NX), dma(NX), dma(NY), dma(NY),
        ],
        compiler_params=pltpu.CompilerParams(
            collective_id=0, has_side_effects=True, vmem_limit_bytes=56 * 2**20),
        cost_estimate=pl.CostEstimate(flops=8 * 10**9, bytes_accessed=5 * 10**6, transcendentals=0),
    )(structure, front, jnp.transpose(factor_front, (0, 2, 1)), factor_border, pivot_inverse)


def solution(mesh):
    return jax.shard_map(
        body,
        mesh=mesh,
        in_specs=(P("row", "col"), P(), P(None, "row", "col"), P(), P(None, "row", None)),
        out_specs=(P(None, "row", "col"), P(None, "row", None), P(None, "row", None)),
        check_vma=False,
    )
```

```python
import functools

import jax
import jax.numpy as jnp
from jax import lax
from jax.experimental import pallas as pl
from jax.experimental.pallas import tpu as pltpu
from jax.sharding import PartitionSpec as P

NX, NY, NZ = 4, 8, 8
SIZES = (NX, NY)
SUPER = 3
BLK = 128
OFFSETS = [(dx, dy) for dx in range(1 - NX // 2, NX // 2 + 1) for dy in range(1 - NY // 2, NY // 2 + 1)]
MESH = pl.DeviceIdType.MESH
F32 = jnp.float32


def gather_plan():
    msgs = []
    for first in range(2):
        n1, n2 = SIZES[first], SIZES[1 - first]
        for j in range(1, n1 // 2 + 1):
            for s in (1, -1):
                msgs.append((j, first, s, j, None, 0))
        for o in range(-(n1 // 2) + 1, n1 // 2 + 1):
            for i in range(1, n2 // 2 + 1):
                for s in (1, -1):
                    msgs.append((abs(o) + i, first, 0, o, s, i))
    return msgs


MSGS = gather_plan()
INDEX = {m[1:]: i for i, m in enumerate(MSGS)}
BY_KEY = {m[1:]: m for m in MSGS}


def wrap(v, n):
    return lax.rem(v + n, n)


def split(v):
    high = v.astype(jnp.bfloat16)
    low = (v - high.astype(F32)).astype(jnp.bfloat16)
    return high, low


NN = (((1,), (0,)), ((), ()))
NT = (((1,), (1,)), ((), ()))


def dot3(a, b, dims=NN):
    def one(p, q):
        return lax.dot_general(p, q, dims, preferred_element_type=F32)
    return one(a[0], b[0]) + (one(a[0], b[1]) + one(a[1], b[0]))


def kernel(flag_ref, a_ref, f_ref, b_ref, p_ref, x_out, par_out, d_out,
           FA, FB, PF, Yp, E, RB, Hc, Ah, Al, Bh, Bl, BTh, BTl, Hh, Hl, Yr, TP, R1, R2, R3, TF, U, Q,
           ag_s, ag_r, pz_s, pz_r, ex_s, ex_r, rs_s, rs_r, bc_s, bc_r, rt_s, rt_r, sx_s, sx_r, cp_s,
           t1_s, t1_r, t2_s, t2_r):
    row = lax.axis_index("row")
    col = lax.axis_index("col")
    z, core = lax.div(row, 2), lax.rem(row, 2)
    x, y = lax.div(col, NY), lax.rem(col, NY)
    other = 1 - core

    def at(dx=0, dy=0, dz=0):
        return (wrap(z + dz, NZ) * 2 + core, wrap(x + dx, NX) * NY + wrap(y + dy, NY))

    sibling = (z * 2 + other, col)

    def remote(src, dst, s_sem, r_sem, dev):
        return pltpu.make_async_remote_copy(
            src_ref=src, dst_ref=dst, send_sem=s_sem, recv_sem=r_sem, device_id=dev, device_id_type=MESH)

    sends = []

    def start(c):
        c.start()
        sends.append(c)

    barrier = pltpu.get_barrier_semaphore()
    peers = [(row, wrap(col + o, NX * NY)) for o in range(1, NX * NY)]
    peers += [at(dz=1), at(dz=-1), sibling]
    for dev in peers:
        pl.semaphore_signal(barrier, inc=1, device_id=dev, device_id_type=MESH)

    for k in range(SUPER):
        for j in range(6):
            flag = flag_ref[k, row * 6 + j].astype(F32)
            dst = (FA, FB)[j // 3]
            dst[k, x, y, :, (j % 3) * BLK:(j % 3 + 1) * BLK] = f_ref[k, :, j * BLK:(j + 1) * BLK] * flag
    PF[:, z, core] = p_ref[0:2]
    TP[96:128] = jnp.zeros((32, 512), F32)
    pl.semaphore_wait(barrier, len(peers))

    def ag_copy(key, back):
        first, s1, o, s2, i = key
        n1, n2 = SIZES[first], SIZES[1 - first]
        F = (FA, FB)[first]
        if s2 is None:
            half, s = o == n1 // 2, s1
            off1, off2 = -s1 * (o - 1 + back), 0
            step = (s, 0)
        else:
            half, s = i == n2 // 2, s2
            off1, off2 = o, -s2 * (i - 1 + back)
            step = (0, s)
        rows = pl.ds(0 if s > 0 else 8, 8) if half else pl.ds(0, 16)
        if first == 1:
            off1, off2 = off2, off1
            step = step[::-1]
        ref = F.at[:, wrap(x + off1, NX), wrap(y + off2, NY), rows]
        n = INDEX[key]
        return remote(ref, ref, ag_s.at[n], ag_r.at[n], at(*step))

    def ag_second(first, o):
        o = o if o > -(SIZES[first] // 2) else -o
        for s in (1, -1):
            start(ag_copy((first, 0, o, s, 1), 0))

    def ag_begin():
        for first in range(2):
            for s in (1, -1):
                start(ag_copy((first, s, 1, None, 0), 0))
        for first in range(2):
            ag_second(first, 0)

    def ag_arrive(m):
        key = m[1:]
        ag_copy(key, 1).wait_recv()
        first, s1, o, s2, i = key
        n1, n2 = SIZES[first], SIZES[1 - first]
        if s2 is None:
            if o < n1 // 2:
                start(ag_copy((first, s1, o + 1, None, 0), 0))
                ag_second(first, -s1 * o)
            elif s1 < 0:
                ag_second(first, o)
        elif i < n2 // 2:
            start(ag_copy((first, 0, o, s2, i + 1), 0))

    def ag_tick(t):
        for m in sorted((m for m in MSGS if m[0] == t), key=lambda m: (m[4] is not None, m[5])):
            ag_arrive(m)

    def pz_copy(s, t, back):
        half = t == NZ // 2
        rows = pl.ds(0 if s > 0 else 16, 16) if half else pl.ds(0, 32)
        ref = PF.at[:, wrap(z - s * (t - 1 + back), NZ), core, rows]
        n = (t - 1) * 2 + (s > 0)
        return remote(ref, ref, pz_s.at[n], pz_r.at[n], at(dz=s))

    def pz_tick(t):
        for s in (1, -1):
            if t > 0:
                pz_copy(s, t, 1).wait_recv()
            if t < NZ // 2:
                start(pz_copy(s, t + 1, 0))

    def pz_pair(side):
        ref = PF.at[:, :, side]
        return remote(ref, ref, pz_s.at[8], pz_r.at[8], sibling)

    def prepare():
        Ah[...], Al[...] = split(a_ref[...])
        for i in range(2):
            b = b_ref[i]
            Bh[i], Bl[i] = split(b)
            BTh[i], BTl[i] = split(b.T)

    def product(k):
        for h in range(2):
            out = None
            for F, base in ((FA, 0), (FB, 384)):
                left = split(F[k, 2 * h:2 * h + 2].reshape(256, 384))
                term = dot3(left, (Ah[base:base + 384], Al[base:base + 384]))
                out = term if out is None else out + term
            if k > 0:
                rows = slice(h * 256, h * 256 + 256)
                before = split(Yp[k - 1].reshape(512, 384))
                out = out - dot3((BTh[k - 1, rows], BTl[k - 1, rows]), before)
            Yp[k, 4 * h:4 * h + 4] = out.reshape(4, 2, 32, 384)

    def ex_copy(k):
        return remote(Yp.at[k, :, other], E.at[k], ex_s.at[k], ex_r.at[k], sibling)

    def ex_finish(k):
        ex_copy(k).wait_recv()
        E[k] = E[k] + Yp[k, :, core]

    def rs_rows(s, t):
        return (pl.ds(0, 16) if s > 0 else pl.ds(16, 16)) if t == 1 else pl.ds(0, 32)

    def rs_copy(k, s, t):
        n = (k * 4 + t - 1) * 2 + (s > 0)
        rows = rs_rows(s, t)
        return remote(E.at[k, wrap(z + s * (5 - t), NZ), rows], RB.at[k, int(s > 0), t - 1, rows],
                      rs_s.at[n], rs_r.at[n], at(dz=s))

    def rs_tick(k, t):
        for s in (1, -1):
            if t > 0:
                rs_copy(k, s, t).wait_recv()
                rows = rs_rows(s, t)
                block = wrap(z + s * (4 - t), NZ)
                E[k, block, rows] = E[k, block, rows] + RB[k, int(s > 0), t - 1, rows]
            if t < 4:
                start(rs_copy(k, s, t + 1))

    def columns_out(k):
        image = E[k, z]
        Yr[k] = image
        for j in range(3):
            flag = flag_ref[k, col * 3 + j].astype(F32)
            lanes = slice(j * BLK, (j + 1) * BLK)
            x_out[k, :, lanes] = -(image[:, lanes] * flag)

    root_z = lax.div(col, 4)
    root_core = lax.rem(lax.div(col, 2), 2)
    in_root_plane = z == root_z
    is_root = jnp.logical_and(in_root_plane, core == root_core)
    is_twin = jnp.logical_and(in_root_plane, core != root_core)
    even = lax.rem(col, 2) == 0
    from_root = wrap(z - root_z, NZ)
    half_rows = pl.ds(pl.multiple_of(core * 8, 8), 8)

    def spread(group, act):
        for F, mine in ((FA, even), (FB, jnp.logical_not(even))):
            @pl.when(jnp.logical_and(is_root, mine))
            def _():
                for n, d, xi, yi in group:
                    act(remote(F.at[:, xi, yi], Hc.at[:, xi, yi], rt_s.at[n], rt_r.at[n], sibling), None)
                    act(remote(F.at[:, xi, yi, half_rows], Hc.at[:, xi, yi, half_rows],
                               bc_s.at[n], bc_r.at[n], at(dz=d)), None)

        @pl.when(is_twin)
        def _():
            for n, d, xi, yi in group:
                whole = Hc.at[:, xi, yi]
                part = Hc.at[:, xi, yi, half_rows]
                act(remote(part, part, bc_s.at[n], bc_r.at[n], at(dz=d)),
                    remote(whole, whole, rt_s.at[n], rt_r.at[n], sibling))

    def hand_on(group, h, act):
        for way in (1, -1):
            @pl.when(from_root == (h if way > 0 else NZ - h))
            def _():
                for n, d, xi, yi in group:
                    if d == way:
                        part = Hc.at[:, xi, yi, half_rows]
                        c = remote(part, part, bc_s.at[n], bc_r.at[n], at(dz=d))
                        act(c if h < NZ - 1 else None, c)

    def bc_go(c, before):
        if before is not None:
            before.wait_recv()
        if c is not None:
            c.start()

    def bc_end(c, before):
        if c is not None:
            c.wait_send()

    def bc_group(t):
        return [(n, (1, -1)[(dx + dy) // 2 % 2] if (dx + dy) % 2 == 0 else (1, -1)[(dx - dy + 1) // 2 % 2], wrap(x + dx + NX, NX), wrap(y + dy + NY, NY))
                for n, (dx, dy) in enumerate(OFFSETS) if abs(dx) + abs(dy) == t]

    def bc_step(g, act=bc_go):
        for h in range(NZ - 1, -1, -1):
            if 0 <= g - h <= 6:
                group = bc_group(g - h)
                spread(group, act) if h == 0 else hand_on(group, h, act)

    def bc_local(act):
        for F, mine in ((FA, even), (FB, jnp.logical_not(even))):
            @pl.when(jnp.logical_and(is_root, mine))
            def _():
                cp = pltpu.make_async_copy(F, Hc, cp_s.at[0])
                cp.start() if act == "start" else cp.wait()

    def bc_pair(side):
        ref = Hc.at[:, :, :, pl.ds(pl.multiple_of(side * 8, 8), 8)]
        return remote(ref, ref, sx_s.at[0], sx_r.at[0], sibling)

    def bc_swap():
        @pl.when(jnp.logical_not(in_root_plane))
        def _():
            bc_pair(core).start()

    def bc_swapped():
        @pl.when(jnp.logical_not(in_root_plane))
        def _():
            bc_pair(other).wait_recv()
            bc_pair(core).wait_send()
        bc_local("wait")

    def reduced_factor(k):
        h = Hc[k].reshape(512, 384)
        if k > 0:
            h = h - dot3((BTh[k - 1], BTl[k - 1]), (Hh[k - 1], Hl[k - 1]))
        Hh[k], Hl[k] = split(h)

    def gram(k):
        if k == 0:
            TP[0:32] = dot3(split(Yr[0]), (Hh[0], Hl[0]), NT)
        else:
            left = Yr[k - 1:k + 1].reshape(64, 384)
            base = 32 if k == 1 else 128
            TP[base:base + 64] = dot3(split(left), (Hh[k], Hl[k]), NT)

    COLS = NX * NY
    BATCH = ((0, 16), (128, 8))

    def piece_of(b, at_col):
        base, n = BATCH[b]
        return TP.at[pl.ds(pl.multiple_of(base + lax.div(at_col, 4) * n, 8), n),
                     pl.ds(pl.multiple_of(lax.rem(at_col, 4) * BLK, BLK), BLK)]

    def at_col(o):
        return (row, wrap(col + o, COLS))

    def slots_of(buf, b):
        return buf.at[b, pl.ds(1, COLS - 1), pl.ds(0, BATCH[b][1])]

    def t_wait(buf, s_sem, r_sem, b, what):
        c = remote(slots_of(buf, b), slots_of(buf, b), s_sem.at[b], r_sem.at[b], at_col(1))
        getattr(c, what)()

    def t_first(b):
        for o in range(1, COLS):
            remote(piece_of(b, wrap(col + o, COLS)), R1.at[b, o, pl.ds(0, BATCH[b][1])],
                   t1_s.at[b], t1_r.at[b], at_col(o)).start()

    def t_second(b):
        rows = pl.ds(0, BATCH[b][1])
        own = piece_of(b, col)[...]
        t_wait(R1, t1_s, t1_r, b, "wait_recv")
        parts = [own] + [R1[b, o, rows] for o in range(1, COLS)]
        while len(parts) > 1:
            parts = [p + q for p, q in zip(parts[::2], parts[1::2])]
        R3[b, rows] = parts[0]
        for o in range(1, COLS):
            remote(R3.at[b, rows], R2.at[b, o, rows], t2_s.at[b], t2_r.at[b], at_col(o)).start()
        R2[b, 0, rows] = parts[0]

    def t_last(b):
        base, n = BATCH[b]
        t_wait(R2, t2_s, t2_r, b, "wait_recv")
        for i in range(COLS):
            TF[base + i // 4 * n:base + i // 4 * n + n, i % 4 * BLK:i % 4 * BLK + BLK] = R2[b, wrap(col - i + COLS, COLS), 0:n]

    def t_end(b):
        t_wait(R1, t1_s, t1_r, b, "wait_send")
        t_wait(R2, t2_s, t2_r, b, "wait_send")

    def drain():
        for c in sends:
            c.wait_send()
        sends.clear()

    def pivot_terms():
        b0, b1 = (Bh[0], Bl[0]), (Bh[1], Bl[1])
        mine = pl.ds(pl.multiple_of(row * 32, 32), 32)
        bt0, bt1 = (BTh[0, mine], BTl[0, mine]), (BTh[1, mine], BTl[1, mine])
        p0, p1 = split(PF[0].reshape(512, 512)), split(PF[1].reshape(512, 512))
        own0, own1, own2 = p_ref[0], p_ref[1], p_ref[2]
        q1 = own1 + dot3(split(dot3(bt0, p0, NT)), b0)
        U[0] = dot3(split(own0), b0)
        U[1] = dot3(split(q1), b1)
        inner = dot3(split(dot3(split(dot3(bt1, b0, NT)), p0)), b0) + dot3(bt1, p1, NT)
        Q[0] = q1
        Q[1] = own2 + dot3(split(inner), b1)

    ag_begin()
    pz_tick(0)
    bc_step(0)
    prepare()
    for g in range(1, 7):
        ag_tick(g)
        if g <= 4:
            pz_tick(g)
        if g == 5:
            start(pz_pair(core))
        bc_step(g)
    bc_local("start")
    product(0)
    start(ex_copy(0))
    bc_step(7)
    product(1)
    start(ex_copy(1))
    ex_finish(0)
    rs_tick(0, 0)
    bc_step(8)
    product(2)
    start(ex_copy(2))
    rs_tick(0, 1)
    ex_finish(1)
    rs_tick(1, 0)
    bc_step(9)
    rs_tick(0, 2)
    rs_tick(1, 1)
    ex_finish(2)
    rs_tick(2, 0)
    bc_step(10)
    rs_tick(0, 3)
    rs_tick(1, 2)
    rs_tick(2, 1)
    bc_step(11)
    rs_tick(0, 4)
    rs_tick(1, 3)
    rs_tick(2, 2)
    bc_step(12)
    bc_step(13)
    bc_swap()
    columns_out(0)
    pz_pair(other).wait_recv()
    pivot_terms()
    rs_tick(1, 4)
    rs_tick(2, 3)
    bc_swapped()
    reduced_factor(0)
    gram(0)
    reduced_factor(1)
    columns_out(1)
    gram(1)
    t_first(0)
    reduced_factor(2)
    rs_tick(2, 4)
    columns_out(2)
    gram(2)
    t_first(1)
    t_second(0)
    drain()
    for g in range(14):
        bc_step(g, bc_end)
    t_second(1)
    t_last(0)
    d_out[0] = p_ref[0] + TF[0:32]
    par_out[0] = TF[32:64] - U[0]
    d_out[1] = Q[0] + TF[64:96]
    t_last(1)
    par_out[1] = TF[128:160] - U[1]
    d_out[2] = Q[1] + TF[160:192]
    t_end(0)
    t_end(1)


def deliver(*refs):
    for src, dst in zip(refs[:3], refs[3:]):
        dst[...] = src[...]


def body(front, structure, factor_front, factor_border, pivot_inverse):
    vmem = pl.BlockSpec(memory_space=pltpu.VMEM)
    dma = lambda n: pltpu.SemaphoreType.DMA((n,))
    v = lambda *shape: pltpu.VMEM(shape, F32)
    h = lambda *shape: pltpu.VMEM(shape, jnp.bfloat16)
    n_ag = len(MSGS)
    shapes = (
        jax.ShapeDtypeStruct((3, 32, 384), F32),
        jax.ShapeDtypeStruct((2, 32, 512), F32),
        jax.ShapeDtypeStruct((3, 32, 512), F32),
    )
    results = pl.pallas_call(
        kernel,
        out_shape=shapes,
        in_specs=[pl.BlockSpec(memory_space=pltpu.SMEM)] + [vmem] * 4,
        out_specs=(vmem,) * 3,
        scratch_shapes=[
            v(3, NX, NY, 16, 384), v(3, NX, NY, 16, 384),
            v(2, NZ, 2, 32, 512),
            v(3, NZ, 2, 32, 384),
            v(3, NZ, 32, 384),
            v(3, 2, 4, 32, 384),
            v(3, NX, NY, 16, 384),
            h(768, 384), h(768, 384),
            h(2, 512, 512), h(2, 512, 512), h(2, 512, 512), h(2, 512, 512),
            h(3, 512, 384), h(3, 512, 384),
            v(3, 32, 384),
            v(192, 512),
            v(2, 32, 16, 128), v(2, 32, 16, 128), v(2, 16, 128),
            v(192, 512),
            v(2, 32, 512), v(2, 32, 512),
            dma(n_ag), dma(n_ag),
            dma(9), dma(9),
            dma(3), dma(3),
            dma(24), dma(24),
            dma(32), dma(32),
            dma(32), dma(32),
            dma(1), dma(1),
            dma(1),
            dma(2), dma(2), dma(2), dma(2),
        ],
        compiler_params=pltpu.CompilerParams(
            collective_id=0, has_side_effects=True, vmem_limit_bytes=56 * 2**20),
        cost_estimate=pl.CostEstimate(flops=8 * 10**9, bytes_accessed=5 * 10**6, transcendentals=0),
    )(structure, front, jnp.transpose(factor_front, (0, 2, 1)), factor_border, pivot_inverse)
    return pl.pallas_call(deliver, out_shape=shapes, in_specs=[vmem] * 3, out_specs=(vmem,) * 3)(*results)


def solution(mesh):
    return jax.shard_map(
        body,
        mesh=mesh,
        in_specs=(P("row", "col"), P(), P(None, "row", "col"), P(), P(None, "row", None)),
        out_specs=(P(None, "row", "col"), P(None, "row", None), P(None, "row", None)),
        check_vma=False,
    )
```

```python
import functools

import jax
import jax.numpy as jnp
from jax import lax
from jax.experimental import pallas as pl
from jax.experimental.pallas import tpu as pltpu
from jax.sharding import PartitionSpec as P

NX, NY, NZ = 4, 8, 8
SIZES = (NX, NY)
SUPER = 3
BLK = 128
OFFSETS = [(dx, dy) for dx in range(1 - NX // 2, NX // 2 + 1) for dy in range(1 - NY // 2, NY // 2 + 1)]
MESH = pl.DeviceIdType.MESH
F32 = jnp.float32


def gather_plan():
    msgs = []
    for first in range(2):
        n1, n2 = SIZES[first], SIZES[1 - first]
        for j in range(1, n1 // 2 + 1):
            for s in (1, -1):
                msgs.append((j, first, s, j, None, 0))
        for o in range(-(n1 // 2) + 1, n1 // 2 + 1):
            for i in range(1, n2 // 2 + 1):
                for s in (1, -1):
                    msgs.append((abs(o) + i, first, 0, o, s, i))
    return msgs


MSGS = gather_plan()
INDEX = {m[1:]: i for i, m in enumerate(MSGS)}
BY_KEY = {m[1:]: m for m in MSGS}


def wrap(v, n):
    return lax.rem(v + n, n)


def split(v):
    high = v.astype(jnp.bfloat16)
    low = (v - high.astype(F32)).astype(jnp.bfloat16)
    return high, low


NN = (((1,), (0,)), ((), ()))
NT = (((1,), (1,)), ((), ()))


def dot3(a, b, dims=NN):
    def one(p, q):
        return lax.dot_general(p, q, dims, preferred_element_type=F32)
    return one(a[0], b[0]) + (one(a[0], b[1]) + one(a[1], b[0]))


def kernel(flag_ref, a_ref, f_ref, b_ref, p_ref, x_out, par_out, d_out,
           FA, FB, PF, Yp, E, RB, Hc, Ah, Al, Bh, Bl, BTh, BTl, Hh, Hl, Yr, TP, R1, R2, R3, TF, U, Q,
           ag_s, ag_r, pz_s, pz_r, ex_s, ex_r, rs_s, rs_r, bc_s, bc_r, rt_s, rt_r, sx_s, sx_r, cp_s,
           t1_s, t1_r, t2_s, t2_r):
    row = lax.axis_index("row")
    col = lax.axis_index("col")
    z, core = lax.div(row, 2), lax.rem(row, 2)
    x, y = lax.div(col, NY), lax.rem(col, NY)
    other = 1 - core

    def at(dx=0, dy=0, dz=0):
        return (wrap(z + dz, NZ) * 2 + core, wrap(x + dx, NX) * NY + wrap(y + dy, NY))

    sibling = (z * 2 + other, col)

    def remote(src, dst, s_sem, r_sem, dev):
        return pltpu.make_async_remote_copy(
            src_ref=src, dst_ref=dst, send_sem=s_sem, recv_sem=r_sem, device_id=dev, device_id_type=MESH)

    sends = []

    def start(c):
        c.start()
        sends.append(c)

    barrier = pltpu.get_barrier_semaphore()
    peers = [(row, wrap(col + o, NX * NY)) for o in range(1, NX * NY)]
    peers += [at(dz=1), at(dz=-1), sibling]
    for dev in peers:
        pl.semaphore_signal(barrier, inc=1, device_id=dev, device_id_type=MESH)

    for k in range(SUPER):
        for j in range(6):
            flag = flag_ref[k, row * 6 + j].astype(F32)
            dst = (FA, FB)[j // 3]
            dst[k, x, y, :, (j % 3) * BLK:(j % 3 + 1) * BLK] = f_ref[k, :, j * BLK:(j + 1) * BLK] * flag
    PF[:, z, core] = p_ref[0:2]
    TP[96:128] = jnp.zeros((32, 512), F32)
    pl.semaphore_wait(barrier, len(peers))

    def ag_copy(key, back):
        first, s1, o, s2, i = key
        n1, n2 = SIZES[first], SIZES[1 - first]
        F = (FA, FB)[first]
        if s2 is None:
            half, s = o == n1 // 2, s1
            off1, off2 = -s1 * (o - 1 + back), 0
            step = (s, 0)
        else:
            half, s = i == n2 // 2, s2
            off1, off2 = o, -s2 * (i - 1 + back)
            step = (0, s)
        rows = pl.ds(0 if s > 0 else 8, 8) if half else pl.ds(0, 16)
        if first == 1:
            off1, off2 = off2, off1
            step = step[::-1]
        ref = F.at[:, wrap(x + off1, NX), wrap(y + off2, NY), rows]
        n = INDEX[key]
        return remote(ref, ref, ag_s.at[n], ag_r.at[n], at(*step))

    def ag_second(first, o):
        o = o if o > -(SIZES[first] // 2) else -o
        for s in (1, -1):
            start(ag_copy((first, 0, o, s, 1), 0))

    def ag_begin():
        for first in range(2):
            for s in (1, -1):
                start(ag_copy((first, s, 1, None, 0), 0))
        for first in range(2):
            ag_second(first, 0)

    def ag_arrive(m):
        key = m[1:]
        ag_copy(key, 1).wait_recv()
        first, s1, o, s2, i = key
        n1, n2 = SIZES[first], SIZES[1 - first]
        if s2 is None:
            if o < n1 // 2:
                start(ag_copy((first, s1, o + 1, None, 0), 0))
                ag_second(first, -s1 * o)
            elif s1 < 0:
                ag_second(first, o)
        elif i < n2 // 2:
            start(ag_copy((first, 0, o, s2, i + 1), 0))

    def ag_tick(t):
        for m in sorted((m for m in MSGS if m[0] == t), key=lambda m: (m[4] is not None, m[5])):
            ag_arrive(m)

    def pz_copy(s, t, back):
        half = t == NZ // 2
        rows = pl.ds(0 if s > 0 else 16, 16) if half else pl.ds(0, 32)
        ref = PF.at[:, wrap(z - s * (t - 1 + back), NZ), core, rows]
        n = (t - 1) * 2 + (s > 0)
        return remote(ref, ref, pz_s.at[n], pz_r.at[n], at(dz=s))

    def pz_tick(t):
        for s in (1, -1):
            if t > 0:
                pz_copy(s, t, 1).wait_recv()
            if t < NZ // 2:
                start(pz_copy(s, t + 1, 0))

    def pz_pair(side):
        ref = PF.at[:, :, side]
        return remote(ref, ref, pz_s.at[8], pz_r.at[8], sibling)

    def prepare():
        Ah[...], Al[...] = split(a_ref[...])
        for i in range(2):
            b = b_ref[i]
            Bh[i], Bl[i] = split(b)
            BTh[i], BTl[i] = split(b.T)

    def product(k):
        for h in range(2):
            out = None
            for F, base in ((FA, 0), (FB, 384)):
                left = split(F[k, 2 * h:2 * h + 2].reshape(256, 384))
                term = dot3(left, (Ah[base:base + 384], Al[base:base + 384]))
                out = term if out is None else out + term
            if k > 0:
                rows = slice(h * 256, h * 256 + 256)
                before = split(Yp[k - 1].reshape(512, 384))
                out = out - dot3((BTh[k - 1, rows], BTl[k - 1, rows]), before)
            Yp[k, 4 * h:4 * h + 4] = out.reshape(4, 2, 32, 384)

    def ex_copy(k):
        return remote(Yp.at[k, :, other], E.at[k], ex_s.at[k], ex_r.at[k], sibling)

    def ex_finish(k):
        ex_copy(k).wait_recv()
        E[k] = E[k] + Yp[k, :, core]

    def rs_rows(s, t):
        return (pl.ds(0, 16) if s > 0 else pl.ds(16, 16)) if t == 1 else pl.ds(0, 32)

    def rs_copy(k, s, t):
        n = (k * 4 + t - 1) * 2 + (s > 0)
        rows = rs_rows(s, t)
        return remote(E.at[k, wrap(z + s * (5 - t), NZ), rows], RB.at[k, int(s > 0), t - 1, rows],
                      rs_s.at[n], rs_r.at[n], at(dz=s))

    def rs_tick(k, t):
        for s in (1, -1):
            if t > 0:
                rs_copy(k, s, t).wait_recv()
                rows = rs_rows(s, t)
                block = wrap(z + s * (4 - t), NZ)
                E[k, block, rows] = E[k, block, rows] + RB[k, int(s > 0), t - 1, rows]
            if t < 4:
                start(rs_copy(k, s, t + 1))

    def columns_out(k):
        image = E[k, z]
        Yr[k] = image
        for j in range(3):
            flag = flag_ref[k, col * 3 + j].astype(F32)
            lanes = slice(j * BLK, (j + 1) * BLK)
            x_out[k, :, lanes] = -(image[:, lanes] * flag)

    root_z = lax.div(col, 4)
    root_core = lax.rem(lax.div(col, 2), 2)
    in_root_plane = z == root_z
    is_root = jnp.logical_and(in_root_plane, core == root_core)
    is_twin = jnp.logical_and(in_root_plane, core != root_core)
    even = lax.rem(col, 2) == 0
    from_root = wrap(z - root_z, NZ)
    hop = jnp.minimum(from_root, NZ - from_root)
    onward = jnp.where(from_root < NZ // 2, 1, -1)
    half_rows = pl.ds(pl.multiple_of(core * 8, 8), 8)

    def spread(group, act):
        for F, mine in ((FA, even), (FB, jnp.logical_not(even))):
            @pl.when(jnp.logical_and(is_root, mine))
            def _():
                for n, xi, yi in group:
                    act(remote(F.at[:, xi, yi], Hc.at[:, xi, yi], rt_s.at[n], rt_r.at[n], sibling), None)
                for n, xi, yi in group:
                    for d in (1, -1):
                        act(remote(F.at[:, xi, yi, half_rows], Hc.at[:, xi, yi, half_rows],
                                   bc_s.at[n * 2 + (d > 0)], bc_r.at[n], at(dz=d)), None)

        @pl.when(is_twin)
        def _():
            for n, xi, yi in group:
                whole = Hc.at[:, xi, yi]
                part = Hc.at[:, xi, yi, half_rows]
                for d in (1, -1):
                    act(remote(part, part, bc_s.at[n * 2 + (d > 0)], bc_r.at[n], at(dz=d)),
                        remote(whole, whole, rt_s.at[n], rt_r.at[n], sibling) if d > 0 else None)

    def hand_on(group, h, act):
        def run(forward):
            for n, xi, yi in group:
                part = Hc.at[:, xi, yi, half_rows]
                c = remote(part, part, bc_s.at[n * 2], bc_r.at[n], at(dz=onward))
                act(c if forward else None, c)
        if h < 3:
            pl.when(hop == h)(lambda: run(True))
        elif h == 3:
            pl.when(from_root == 3)(lambda: run(True))
            pl.when(from_root == NZ - 3)(lambda: run(False))
        else:
            pl.when(hop == h)(lambda: run(False))

    def bc_go(c, before):
        if before is not None:
            before.wait_recv()
        if c is not None:
            c.start()

    def bc_end(c, before):
        if c is not None:
            c.wait_send()

    def bc_group(t):
        return [(n, wrap(x + dx + NX, NX), wrap(y + dy + NY, NY))
                for n, (dx, dy) in enumerate(OFFSETS) if abs(dx) + abs(dy) == t]

    def bc_step(g, act=bc_go):
        for h in range(NZ // 2, -1, -1):
            if 0 <= g - h <= 6:
                group = bc_group(g - h)
                spread(group, act) if h == 0 else hand_on(group, h, act)

    def bc_local(act):
        for F, mine in ((FA, even), (FB, jnp.logical_not(even))):
            @pl.when(jnp.logical_and(is_root, mine))
            def _():
                cp = pltpu.make_async_copy(F, Hc, cp_s.at[0])
                cp.start() if act == "start" else cp.wait()

    def bc_pair(side):
        ref = Hc.at[:, :, :, pl.ds(pl.multiple_of(side * 8, 8), 8)]
        return remote(ref, ref, sx_s.at[0], sx_r.at[0], sibling)

    def bc_swap():
        @pl.when(jnp.logical_not(in_root_plane))
        def _():
            bc_pair(core).start()

    def bc_swapped():
        @pl.when(jnp.logical_not(in_root_plane))
        def _():
            bc_pair(other).wait_recv()
            bc_pair(core).wait_send()
        bc_local("wait")

    def reduced_factor(k):
        h = Hc[k].reshape(512, 384)
        if k > 0:
            h = h - dot3((BTh[k - 1], BTl[k - 1]), (Hh[k - 1], Hl[k - 1]))
        Hh[k], Hl[k] = split(h)

    def gram(k):
        if k == 0:
            TP[0:32] = dot3(split(Yr[0]), (Hh[0], Hl[0]), NT)
        else:
            left = Yr[k - 1:k + 1].reshape(64, 384)
            base = 32 if k == 1 else 128
            TP[base:base + 64] = dot3(split(left), (Hh[k], Hl[k]), NT)

    COLS = NX * NY
    BATCH = ((0, 16), (128, 8))

    def piece_of(b, at_col):
        base, n = BATCH[b]
        return TP.at[pl.ds(pl.multiple_of(base + lax.div(at_col, 4) * n, 8), n),
                     pl.ds(pl.multiple_of(lax.rem(at_col, 4) * BLK, BLK), BLK)]

    def at_col(o):
        return (row, wrap(col + o, COLS))

    def slots_of(buf, b):
        return buf.at[b, pl.ds(1, COLS - 1), pl.ds(0, BATCH[b][1])]

    def t_wait(buf, s_sem, r_sem, b, what):
        c = remote(slots_of(buf, b), slots_of(buf, b), s_sem.at[b], r_sem.at[b], at_col(1))
        getattr(c, what)()

    def t_first(b):
        for o in range(1, COLS):
            remote(piece_of(b, wrap(col + o, COLS)), R1.at[b, o, pl.ds(0, BATCH[b][1])],
                   t1_s.at[b], t1_r.at[b], at_col(o)).start()

    def t_second(b):
        rows = pl.ds(0, BATCH[b][1])
        own = piece_of(b, col)[...]
        t_wait(R1, t1_s, t1_r, b, "wait_recv")
        parts = [own] + [R1[b, o, rows] for o in range(1, COLS)]
        while len(parts) > 1:
            parts = [p + q for p, q in zip(parts[::2], parts[1::2])]
        R3[b, rows] = parts[0]
        for o in range(1, COLS):
            remote(R3.at[b, rows], R2.at[b, o, rows], t2_s.at[b], t2_r.at[b], at_col(o)).start()
        R2[b, 0, rows] = parts[0]

    def t_last(b):
        base, n = BATCH[b]
        t_wait(R2, t2_s, t2_r, b, "wait_recv")
        for i in range(COLS):
            TF[base + i // 4 * n:base + i // 4 * n + n, i % 4 * BLK:i % 4 * BLK + BLK] = R2[b, wrap(col - i + COLS, COLS), 0:n]

    def t_end(b):
        t_wait(R1, t1_s, t1_r, b, "wait_send")
        t_wait(R2, t2_s, t2_r, b, "wait_send")

    def drain():
        for c in sends:
            c.wait_send()
        sends.clear()

    def pivot_terms():
        b0, b1 = (Bh[0], Bl[0]), (Bh[1], Bl[1])
        mine = pl.ds(pl.multiple_of(row * 32, 32), 32)
        bt0, bt1 = (BTh[0, mine], BTl[0, mine]), (BTh[1, mine], BTl[1, mine])
        p0, p1 = split(PF[0].reshape(512, 512)), split(PF[1].reshape(512, 512))
        own0, own1, own2 = p_ref[0], p_ref[1], p_ref[2]
        q1 = own1 + dot3(split(dot3(bt0, p0, NT)), b0)
        U[0] = dot3(split(own0), b0)
        U[1] = dot3(split(q1), b1)
        inner = dot3(split(dot3(split(dot3(bt1, b0, NT)), p0)), b0) + dot3(bt1, p1, NT)
        Q[0] = q1
        Q[1] = own2 + dot3(split(inner), b1)

    ag_begin()
    pz_tick(0)
    bc_step(0)
    prepare()
    for g in range(1, 7):
        ag_tick(g)
        if g <= 4:
            pz_tick(g)
        if g == 5:
            start(pz_pair(core))
        bc_step(g)
    bc_local("start")
    product(0)
    start(ex_copy(0))
    bc_step(7)
    product(1)
    start(ex_copy(1))
    ex_finish(0)
    rs_tick(0, 0)
    bc_step(8)
    product(2)
    start(ex_copy(2))
    rs_tick(0, 1)
    ex_finish(1)
    rs_tick(1, 0)
    bc_step(9)
    rs_tick(0, 2)
    rs_tick(1, 1)
    ex_finish(2)
    rs_tick(2, 0)
    bc_step(10)
    bc_swap()
    rs_tick(0, 3)
    rs_tick(1, 2)
    rs_tick(2, 1)
    rs_tick(0, 4)
    rs_tick(1, 3)
    rs_tick(2, 2)
    columns_out(0)
    rs_tick(1, 4)
    rs_tick(2, 3)
    bc_swapped()
    reduced_factor(0)
    gram(0)
    reduced_factor(1)
    columns_out(1)
    gram(1)
    t_first(0)
    reduced_factor(2)
    rs_tick(2, 4)
    columns_out(2)
    gram(2)
    t_first(1)
    t_second(0)
    t_second(1)
    pz_pair(other).wait_recv()
    pivot_terms()
    drain()
    for g in range(11):
        bc_step(g, bc_end)
    t_last(0)
    d_out[0] = p_ref[0] + TF[0:32]
    par_out[0] = TF[32:64] - U[0]
    d_out[1] = Q[0] + TF[64:96]
    t_last(1)
    par_out[1] = TF[128:160] - U[1]
    d_out[2] = Q[1] + TF[160:192]
    t_end(0)
    t_end(1)


def deliver(*refs):
    for src, dst in zip(refs[:3], refs[3:]):
        dst[...] = src[...]


def body(front, structure, factor_front, factor_border, pivot_inverse):
    vmem = pl.BlockSpec(memory_space=pltpu.VMEM)
    dma = lambda n: pltpu.SemaphoreType.DMA((n,))
    v = lambda *shape: pltpu.VMEM(shape, F32)
    h = lambda *shape: pltpu.VMEM(shape, jnp.bfloat16)
    n_ag = len(MSGS)
    shapes = (
        jax.ShapeDtypeStruct((3, 32, 384), F32),
        jax.ShapeDtypeStruct((2, 32, 512), F32),
        jax.ShapeDtypeStruct((3, 32, 512), F32),
    )
    results = pl.pallas_call(
        kernel,
        out_shape=shapes,
        in_specs=[pl.BlockSpec(memory_space=pltpu.SMEM)] + [vmem] * 4,
        out_specs=(vmem,) * 3,
        scratch_shapes=[
            v(3, NX, NY, 16, 384), v(3, NX, NY, 16, 384),
            v(2, NZ, 2, 32, 512),
            v(3, NZ, 2, 32, 384),
            v(3, NZ, 32, 384),
            v(3, 2, 4, 32, 384),
            v(3, NX, NY, 16, 384),
            h(768, 384), h(768, 384),
            h(2, 512, 512), h(2, 512, 512), h(2, 512, 512), h(2, 512, 512),
            h(3, 512, 384), h(3, 512, 384),
            v(3, 32, 384),
            v(192, 512),
            v(2, 32, 16, 128), v(2, 32, 16, 128), v(2, 16, 128),
            v(192, 512),
            v(2, 32, 512), v(2, 32, 512),
            dma(n_ag), dma(n_ag),
            dma(9), dma(9),
            dma(3), dma(3),
            dma(24), dma(24),
            dma(64), dma(32),
            dma(32), dma(32),
            dma(1), dma(1),
            dma(1),
            dma(2), dma(2), dma(2), dma(2),
        ],
        compiler_params=pltpu.CompilerParams(
            collective_id=0, has_side_effects=True, vmem_limit_bytes=56 * 2**20),
        cost_estimate=pl.CostEstimate(flops=8 * 10**9, bytes_accessed=5 * 10**6, transcendentals=0),
    )(structure, front, jnp.transpose(factor_front, (0, 2, 1)), factor_border, pivot_inverse)
    return pl.pallas_call(deliver, out_shape=shapes, in_specs=[vmem] * 3, out_specs=(vmem,) * 3)(*results)


def solution(mesh):
    return jax.shard_map(
        body,
        mesh=mesh,
        in_specs=(P("row", "col"), P(), P(None, "row", "col"), P(), P(None, "row", None)),
        out_specs=(P(None, "row", "col"), P(None, "row", None), P(None, "row", None)),
        check_vma=False,
    )
```
